32 devices in a mesh: shard: 4 (over z), ctx: 4 (over y, core), tp: 2 (over x).
Axes of the slice: x: 2, y: 2, z: 4, core: 2. Of those that a mesh axis runs over, the one named last changes fastest.
Arguments:
- tokens: bfloat16 [32, 1024, 1152], P('shard', 'ctx'), may hold values from -6 to 6
- condition: bfloat16 [32, 1152], P('shard'), may hold values from -3 to 3
- modulate_weight: bfloat16 [1152, 6912], P('shard', 'tp'), may hold values from -0.1875 to 0.1875
- modulate_bias: bfloat16 [6912], P(('tp', 'shard')), may hold values from -0.59765625 to 0.59765625
- project_weight: bfloat16 [1152, 3, 1152], P('shard', None, 'tp'), may hold values from -0.1875 to 0.1875
- project_bias: bfloat16 [2, 1152], P(None, ('tp', 'shard')), may hold values from -0.59765625 to 0.59765625
- output_weight: bfloat16 [1152, 1152], P('tp', 'shard'), may hold values from -1 to 1
- output_bias: bfloat16 [1152], P('shard'), may hold values from -0.59765625 to 0.59765625
- expand_weight: bfloat16 [1152, 4608], P('shard', 'tp'), may hold values from -0.1875 to 0.1875
- expand_bias: bfloat16 [4608], P(('tp', 'shard')), may hold values from -0.59765625 to 0.59765625
- reduce_weight: bfloat16 [4608, 1152], P('tp', 'shard'), may hold values from -0.09375 to 0.09375
- reduce_bias: bfloat16 [1152], P('shard'), may hold values from -0.59765625 to 0.59765625
- cotangent: float32 [32, 1024, 1152], P('shard', 'ctx'), may hold values from -3 to 3
Outputs:
- result: float32 [32, 1024, 1152], P('shard', 'ctx')
- tokens_grad: float32 [32, 1024, 1152], P('shard', 'ctx')
- condition_grad: float32 [32, 1152], P('shard')
- modulate_weight_grad: float32 [1152, 6912], P('shard', 'tp')
- modulate_bias_grad: float32 [6912], P(('tp', 'shard'))
- project_weight_grad: float32 [1152, 3, 1152], P('shard', None, 'tp')
- project_bias_grad: float32 [2, 1152], P(None, ('tp', 'shard'))
- output_weight_grad: float32 [1152, 1152], P('tp', 'shard')
- output_bias_grad: float32 [1152], P('shard')
- expand_weight_grad: float32 [1152, 4608], P('shard', 'tp')
- expand_bias_grad: float32 [4608], P(('tp', 'shard'))
- reduce_weight_grad: float32 [4608, 1152], P('tp', 'shard')
- reduce_bias_grad: float32 [1152], P('shard')
The draws below stay inside these ranges and needn't reach their ends.
All inputs are finite; a program needn't handle non-finite values.
Results may differ from the reference program's by a relative error of at most 0.018.
The reference program's roundings to bfloat16 on the way count: a program that leaves them out, or rounds other values in their place, can miss the bound.
Values may be sent and summed in bfloat16 or wider, within the bound.
A program may use at most 320 MiB of HBM per device.

```python
from functools import partial
import jax
import jax.numpy as jnp
from jax import lax

D = 1152
HEADS = 16
HEAD_DIM = 72
FF = 4608
SEQ = 1024
LATENTS = 32


def shard_levels(key, dims, split, low, largest):
    gain = 1.0
    for axis_at, blocks in split:
        draws = jax.random.uniform(jax.random.fold_in(jax.random.fold_in(key, 6), axis_at), (blocks,), jnp.float32, low / len(split), largest / len(split))
        gain = gain * jnp.repeat(jnp.exp(draws), dims[axis_at] // blocks).reshape((-1,) + (1,) * (len(dims) - 1 - axis_at))
    return gain


def normal_values(stream_key, dims, spread, limit, cuts=(), kind=jnp.bfloat16):
    factor_of = shard_levels(stream_key, dims, cuts, -0.22, 0.18) if cuts else 1.0
    values = jax.random.normal(stream_key, dims, jnp.float32) * spread * factor_of
    return jnp.minimum(jnp.maximum(values, -limit), limit).astype(kind)


def setup_inputs(seed: int = 0) -> dict:
    arg_keys = jax.random.split(jax.random.key(seed), 14)
    tokens = normal_values(arg_keys[0], (LATENTS, SEQ, D), 1.0, 6.0, ((0, 4), (1, 4)))
    condition = normal_values(arg_keys[1], (LATENTS, D), 1.0, 3.0, ((0, 4),))
    modulate_weight = normal_values(arg_keys[2], (D, 6 * D), D ** -0.5, 0.1875, ((0, 4), (1, 2)))
    modulate_bias = jnp.clip(jax.random.uniform(arg_keys[3], (6 * D,), jnp.float32, -0.59765625, 0.59765625) * shard_levels(arg_keys[3], (6 * D,), ((0, 8),), -0.4, 0.0), -0.59765625, 0.59765625).astype(jnp.bfloat16)
    project_weight = normal_values(arg_keys[4], (D, 3, D), D ** -0.5, 0.1875, ((0, 4), (2, 2)))
    project_bias = jnp.clip(jax.random.uniform(arg_keys[5], (2, D), jnp.float32, -0.59765625, 0.59765625) * shard_levels(arg_keys[5], (2, D), ((1, 8),), -0.4, 0.0), -0.59765625, 0.59765625).astype(jnp.bfloat16)
    output_weight = normal_values(arg_keys[6], (D, D), (HEAD_DIM // 2) ** -0.5, 1.0, ((0, 2), (1, 4)))
    output_bias = jnp.clip(jax.random.uniform(arg_keys[7], (D,), jnp.float32, -0.59765625, 0.59765625) * shard_levels(arg_keys[7], (D,), ((0, 4),), -0.4, 0.0), -0.59765625, 0.59765625).astype(jnp.bfloat16)
    expand_weight = normal_values(arg_keys[8], (D, FF), D ** -0.5, 0.1875, ((0, 4), (1, 2)))
    expand_bias = jnp.clip(jax.random.uniform(arg_keys[9], (FF,), jnp.float32, -0.59765625, 0.59765625) * shard_levels(arg_keys[9], (FF,), ((0, 8),), -0.4, 0.0), -0.59765625, 0.59765625).astype(jnp.bfloat16)
    reduce_weight = normal_values(arg_keys[10], (FF, D), FF ** -0.5, 0.09375, ((0, 2), (1, 4)))
    reduce_bias = jnp.clip(jax.random.uniform(arg_keys[11], (D,), jnp.float32, -0.59765625, 0.59765625) * shard_levels(arg_keys[11], (D,), ((0, 4),), -0.4, 0.0), -0.59765625, 0.59765625).astype(jnp.bfloat16)
    cotangent = normal_values(arg_keys[12], (LATENTS, SEQ, D), 1.0, 3.0, ((0, 4), (1, 4)), jnp.float32)
    return dict(tokens=tokens, condition=condition, modulate_weight=modulate_weight, modulate_bias=modulate_bias, project_weight=project_weight, project_bias=project_bias, output_weight=output_weight, output_bias=output_bias, expand_weight=expand_weight, expand_bias=expand_bias, reduce_weight=reduce_weight, reduce_bias=reduce_bias, cotangent=cotangent)


@jax.custom_vjp
def low(v):
    return lax.optimization_barrier(v.astype(jnp.bfloat16)).astype(jnp.float32)

@jax.custom_vjp
def low_back(v):
    return v

def low_keep(v):
    return (low(v), None)

def low_pass(kept, grad):
    return (grad,)

def back_keep(v):
    return (v, None)

def back_low(kept, grad):
    return (low(grad),)
low.defvjp(low_keep, low_pass)
low_back.defvjp(back_keep, back_low)

def matmul(left, right):
    return jnp.dot(left, right, precision=lax.Precision.HIGHEST)

def normalize(rows):
    average = lax.optimization_barrier(jnp.mean(rows, axis=-1, keepdims=True))
    centred = rows - average
    variance = lax.optimization_barrier(jnp.mean(centred * centred, axis=-1, keepdims=True))
    return centred * lax.rsqrt(variance + 1e-06)

def one_latent(item, weights):
    tokens_one, modulation_one = item
    project_weight, project_bias, output_weight, output_bias, expand_weight, expand_bias, reduce_weight, reduce_bias = weights
    shift_one = modulation_one[0]
    scale_one = modulation_one[1]
    gate_one = modulation_one[2]
    shift_two = modulation_one[3]
    scale_two = modulation_one[4]
    gate_two = modulation_one[5]
    hidden_one = low(normalize(tokens_one) * (1.0 + scale_one) + shift_one)
    projected = jnp.einsum('td,dcf->tcf', hidden_one, project_weight, precision=lax.Precision.HIGHEST)
    queries = low_back(low(projected[:, 0] + project_bias[0])).reshape(SEQ, HEADS, HEAD_DIM)
    key_rows = low_back(low(projected[:, 1])).reshape(SEQ, HEADS, HEAD_DIM)
    value_rows = low_back(low(projected[:, 2] + project_bias[1])).reshape(SEQ, HEADS, HEAD_DIM)
    raw_scores = jnp.einsum('qhe,khe->hqk', queries, key_rows, precision=lax.Precision.HIGHEST)
    scores = low_back(raw_scores) * HEAD_DIM ** (-0.5)
    probs = jax.nn.softmax(scores, axis=-1)
    attended = jnp.einsum('hqk,khe->qhe', low(probs), value_rows, precision=lax.Precision.HIGHEST).reshape(SEQ, D)
    attended = low_back(low(attended))
    branch = low_back(matmul(attended, output_weight)) + output_bias
    middle = tokens_one + gate_one * branch
    hidden_after_second = low(normalize(middle) * (1.0 + scale_two) + shift_two)
    inner = low_back(matmul(hidden_after_second, expand_weight)) + expand_bias
    gelu_activations = low(jax.nn.gelu(inner, approximate=True))
    mlp_out = low_back(matmul(gelu_activations, reduce_weight)) + reduce_bias
    return middle + gate_two * mlp_out

def forward(tokens, condition, modulate_weight, modulate_bias, project_weight, project_bias, output_weight, output_bias, expand_weight, expand_bias, reduce_weight, reduce_bias):
    silu_cond = low(jax.nn.silu(condition))
    modulation = low_back(matmul(silu_cond, modulate_weight)) + modulate_bias
    modulation = modulation.reshape(LATENTS, 6, D)
    weights = (project_weight, project_bias, output_weight, output_bias, expand_weight, expand_bias, reduce_weight, reduce_bias)
    return lax.map(jax.checkpoint(partial(one_latent, weights=weights)), (tokens, modulation))

def reference(tokens, condition, modulate_weight, modulate_bias, project_weight, project_bias, output_weight, output_bias, expand_weight, expand_bias, reduce_weight, reduce_bias, cotangent):
    inputs = (tokens.astype(jnp.float32), condition.astype(jnp.float32), modulate_weight.astype(jnp.float32), modulate_bias.astype(jnp.float32), project_weight.astype(jnp.float32), project_bias.astype(jnp.float32), output_weight.astype(jnp.float32), output_bias.astype(jnp.float32), expand_weight.astype(jnp.float32), expand_bias.astype(jnp.float32), reduce_weight.astype(jnp.float32), reduce_bias.astype(jnp.float32))
    result, pull = jax.vjp(forward, *inputs)
    grads = pull(cotangent.astype(jnp.float32))
    return (result, grads[0], grads[1], grads[2], grads[3], grads[4], grads[5], grads[6], grads[7], grads[8], grads[9], grads[10], grads[11])
```

```python
from functools import partial

import jax
import jax.numpy as jnp
from jax import lax
from jax.experimental import pallas as pl
from jax.experimental.pallas import tpu as pltpu
from jax.sharding import PartitionSpec as P

HEAD_DIM = 72


epsilon = 1e-06


def normalize(rows):
    average = jnp.mean(rows, axis=-1, keepdims=True)
    centred = rows - average
    variance = jnp.mean(centred * centred, axis=-1, keepdims=True)
    inverse = lax.rsqrt(variance + epsilon)
    return (centred * inverse, inverse)


def normalize_back(normed, inverse, grad_normed):
    first = jnp.mean(grad_normed, axis=-1, keepdims=True)
    second = jnp.mean(grad_normed * normed, axis=-1, keepdims=True)
    return inverse * (grad_normed - first - normed * second)


GROUPS = 2
QUERY_BLOCK = 256
SCALE = HEAD_DIM ** (-0.5)


def tensor_total(partial_sum):
    count = lax.axis_size("tp")
    own = partial_sum.astype(jnp.bfloat16)
    total = own.astype(jnp.float32)
    for step in range(1, count):
        other = lax.ppermute(own, "tp", [(i, (i + step) % count) for i in range(count)])
        total = total + other.astype(jnp.float32)
    return total


def contract(left, right, left_dim, right_dim):
    return lax.dot_general(
        left, right, (((left_dim,), (right_dim,)), ((), ())), preferred_element_type=jnp.float32
    )


def attend_kernel(query_ref, key_ref, value_ref, mixed_ref, logsum_ref):
    keys = key_ref[0, 0]
    values = value_ref[0, 0]
    total_queries = query_ref.shape[3]
    for start in range(0, total_queries, QUERY_BLOCK):
        span = slice(start, start + QUERY_BLOCK)
        scores = contract(keys, query_ref[0, 0, :, span], 0, 0) * SCALE
        peak = jnp.max(scores, axis=0, keepdims=True)
        raised = jnp.exp(scores - peak)
        totals = jnp.sum(raised, axis=0, keepdims=True)
        mixed = contract(values, raised.astype(jnp.bfloat16), 1, 0)
        mixed_ref[0, 0, :, span] = (mixed / totals).astype(jnp.bfloat16)
        logsum_ref[0, 0, :, span] = peak + jnp.log(totals)


def attend_back_kernel(
    query_ref, key_ref, value_ref, grad_ref, logsum_ref, query_out, key_out, value_out
):
    keys = key_ref[0, 0]
    values = value_ref[0, 0]
    total_queries = query_ref.shape[3]
    key_total = jnp.zeros(keys.shape, jnp.float32)
    value_total = jnp.zeros(keys.shape, jnp.float32)
    for start in range(0, total_queries, QUERY_BLOCK):
        span = slice(start, start + QUERY_BLOCK)
        query = query_ref[0, 0, :, span]
        grad = grad_ref[0, 0, :, span]
        scores = contract(keys, query, 0, 0) * SCALE
        probs = jnp.exp(scores - logsum_ref[0, 0, :, span])
        prob_grad = contract(values, grad, 0, 0)
        row_dot = jnp.sum(probs * prob_grad, axis=0, keepdims=True)
        score_grad = (probs * (prob_grad - row_dot) * SCALE).astype(jnp.bfloat16)
        value_total += contract(grad, probs.astype(jnp.bfloat16), 1, 1)
        key_total += contract(query, score_grad, 1, 1)
        query_out[0, 0, :, span] = contract(keys, score_grad, 1, 0).astype(jnp.bfloat16)
    key_out[0, 0] = key_total.astype(jnp.bfloat16)
    value_out[0, 0] = value_total.astype(jnp.bfloat16)


def head_spec(rows, columns):
    return pl.BlockSpec((1, 1, rows, columns), lambda l, h: (l, h, 0, 0))


def attend(queries, keys, values):
    latents, heads, features, count = queries.shape
    wide = head_spec(features, count)
    thin = head_spec(1, count)
    return pl.pallas_call(
        attend_kernel,
        grid=(latents, heads),
        in_specs=[wide] * 3,
        out_specs=[wide, thin],
        out_shape=[
            jax.ShapeDtypeStruct(queries.shape, jnp.bfloat16),
            jax.ShapeDtypeStruct((latents, heads, 1, count), jnp.float32),
        ],
        compiler_params=pltpu.CompilerParams(vmem_limit_bytes=40 * 2**20),
        cost_estimate=pl.CostEstimate(
            flops=4 * latents * heads * 256 * count * count,
            bytes_accessed=8 * queries.size,
            transcendentals=latents * heads * count * count,
        ),
    )(queries, keys, values)


def attend_back(queries, keys, values, grads, logsum):
    latents, heads, features, count = queries.shape
    wide = head_spec(features, count)
    thin = head_spec(1, count)
    return pl.pallas_call(
        attend_back_kernel,
        grid=(latents, heads),
        in_specs=[wide] * 4 + [thin],
        out_specs=[wide] * 3,
        out_shape=[jax.ShapeDtypeStruct(queries.shape, jnp.bfloat16)] * 3,
        compiler_params=pltpu.CompilerParams(vmem_limit_bytes=40 * 2**20),
        cost_estimate=pl.CostEstimate(
            flops=10 * latents * heads * 256 * count * count,
            bytes_accessed=14 * queries.size,
            transcendentals=latents * heads * count * count,
        ),
    )(queries, keys, values, grads, logsum)


def to_heads(rows_in):
    count = lax.axis_size("ctx")
    me = lax.axis_index("ctx")
    latents, kinds, features, own = rows_in.shape
    split = rows_in.reshape(latents, kinds, count, features // (count * HEAD_DIM), HEAD_DIM, own)
    blocks = []
    for step in range(count):
        piece = lax.dynamic_index_in_dim(split, lax.rem(me + step, count), 2, keepdims=False)
        if step:
            piece = lax.ppermute(piece, "ctx", [(i, (i + step) % count) for i in range(count)])
        blocks.append(piece)
    return jnp.concatenate(blocks, axis=-1)


def from_heads(blocks_in):
    count = lax.axis_size("ctx")
    me = lax.axis_index("ctx")
    latents, kinds, heads, features, total = blocks_in.shape
    own = total // count
    pieces = []
    for step in range(count):
        piece = blocks_in[..., step * own : (step + 1) * own]
        if step:
            piece = lax.ppermute(piece, "ctx", [(i, (i - step) % count) for i in range(count)])
        pieces.append(piece)
    twice = jnp.stack(pieces + pieces[:-1], axis=2)
    placed = lax.dynamic_slice_in_dim(twice, lax.rem(count - me, count), count, 2)
    return placed.reshape(latents, kinds, count * heads * features, own)


def own_piece(total, local, dim, shard_index):
    count = local.shape[dim]
    return lax.dynamic_slice_in_dim(total, shard_index * count, count, dim)


def shards(
    tokens,
    condition,
    modulate_weight,
    modulate_bias,
    project_weight,
    project_bias,
    output_weight,
    output_bias,
    expand_weight,
    expand_bias,
    reduce_weight,
    reduce_bias,
    cotangent,
):
    tp_index = lax.axis_index("tp")
    shard_index = lax.axis_index("shard")
    shard_count = lax.axis_size("shard")
    latents_dev = tokens.shape[0]
    width = tokens.shape[2]
    depth = modulate_weight.shape[0]
    half_columns = modulate_weight.shape[1]
    f32 = jnp.float32

    small = (condition, modulate_bias, project_bias, output_bias, expand_bias, reduce_bias)
    packed = lax.all_gather(
        jnp.concatenate([part.reshape(-1) for part in small]), "shard", axis=0
    )
    offset = 0
    unpacked = []
    for part in small:
        unpacked.append(packed[:, offset : offset + part.size].reshape((shard_count,) + part.shape))
        offset += part.size
    full_condition = unpacked[0].reshape(shard_count * latents_dev, width)
    full_modulate_bias = unpacked[1].reshape(-1)
    full_project_bias = jnp.moveaxis(unpacked[2], 0, 1).reshape(2, -1).astype(f32)
    full_output_bias = unpacked[3].reshape(-1).astype(f32)
    full_expand_bias = unpacked[4].reshape(-1).astype(f32)
    full_reduce_bias = unpacked[5].reshape(-1).astype(f32)

    full_project = lax.all_gather(project_weight, "shard", axis=0, tiled=True)
    full_output = lax.all_gather(output_weight, "shard", axis=1, tiled=True)
    full_expand = lax.all_gather(expand_weight, "shard", axis=0, tiled=True)
    full_reduce = lax.all_gather(reduce_weight, "shard", axis=1, tiled=True)

    silu_cond = jax.nn.silu(full_condition.astype(f32)).astype(jnp.bfloat16)
    own_silu = lax.dynamic_slice_in_dim(silu_cond, shard_index * depth, depth, 1)
    modulate_part = jnp.dot(own_silu, modulate_weight, preferred_element_type=f32)
    modulate_half = lax.psum_scatter(
        modulate_part, "shard", scatter_dimension=0, tiled=True
    ) + full_modulate_bias.astype(f32)
    modulation = lax.all_gather(modulate_half, "tp", axis=1, tiled=True).reshape(
        latents_dev, 6, width
    )

    groups = GROUPS if latents_dev % GROUPS == 0 else 1
    size = latents_dev // groups
    spans = [slice(g * size, (g + 1) * size) for g in range(groups)]
    parts = range(groups)
    mods = [[modulation[s, i][:, None, :] for i in range(6)] for s in spans]
    inputs = [tokens[s].astype(f32) for s in spans]
    cotangents = [cotangent[s] for s in spans]

    normed_one, inverse_one, hidden_one, heads_in = [], [], [], []
    for g in parts:
        normed, inverse = normalize(inputs[g])
        normed_one.append(normed)
        inverse_one.append(inverse)
        hidden_one.append((normed * (1.0 + mods[g][1]) + mods[g][0]).astype(jnp.bfloat16))
        projected = jnp.einsum(
            "lsd,dcf->lcfs", hidden_one[g], full_project, preferred_element_type=f32
        )
        bias = jnp.stack(
            [full_project_bias[0], jnp.zeros_like(full_project_bias[0]), full_project_bias[1]]
        )
        heads_in.append(to_heads((projected + bias[None, :, :, None]).astype(jnp.bfloat16)))

    logsum, attended = [], []
    for g in parts:
        mixed, log_one = attend(heads_in[g][:, 0], heads_in[g][:, 1], heads_in[g][:, 2])
        logsum.append(log_one)
        attended.append(from_heads(mixed[:, None])[:, 0])

    branch, middle, normed_two, inverse_two, hidden_two = [], [], [], [], []
    for g in parts:
        branch.append(
            tensor_total(
                jnp.einsum("lfs,fk->lsk", attended[g], full_output, preferred_element_type=f32)
            )
            + full_output_bias
        )
        middle.append(inputs[g] + mods[g][2] * branch[g])
        normed, inverse = normalize(middle[g])
        normed_two.append(normed)
        inverse_two.append(inverse)
        hidden_two.append((normed * (1.0 + mods[g][4]) + mods[g][3]).astype(jnp.bfloat16))

    mlp_low, expand_low, mlp_out, result, activated, hidden_two_grad = [], [], [], [], [], []
    gate_two_grad, reduce_bias_grad, expand_bias_grad = [], 0.0, 0.0
    expand_weight_grad, reduce_weight_grad = 0.0, 0.0
    for g in parts:
        mlp_grad = cotangents[g] * mods[g][5]
        reduce_bias_grad += jnp.sum(mlp_grad, axis=(0, 1))
        mlp_low.append(mlp_grad.astype(jnp.bfloat16))
        inner = (
            jnp.einsum("lsd,dt->lst", hidden_two[g], full_expand, preferred_element_type=f32)
            + full_expand_bias
        )
        gelu = partial(jax.nn.gelu, approximate=True)
        activated.append(gelu(inner).astype(jnp.bfloat16))
        activated_grad = jnp.einsum(
            "lsd,td->lst", mlp_low[g], full_reduce, preferred_element_type=f32
        )
        unused_value, gelu_pull = jax.vjp(gelu, inner)
        inner_grad = gelu_pull(activated_grad)[0]
        expand_bias_grad += jnp.sum(inner_grad, axis=(0, 1))
        expand_low.append(inner_grad.astype(jnp.bfloat16))
        hidden_two_grad.append(
            tensor_total(
                jnp.einsum("lst,dt->lsd", expand_low[g], full_expand, preferred_element_type=f32)
            )
        )
    for g in parts:
        mlp_out.append(
            tensor_total(
                jnp.einsum("lst,td->lsd", activated[g], full_reduce, preferred_element_type=f32)
            )
            + full_reduce_bias
        )
        result.append(middle[g] + mods[g][5] * mlp_out[g])
        gate_two_grad.append(jnp.sum(cotangents[g] * mlp_out[g], axis=1))
        expand_weight_grad += jnp.einsum(
            "lsd,lst->dt", hidden_two[g], expand_low[g], preferred_element_type=f32
        )
        reduce_weight_grad += jnp.einsum(
            "lst,lsd->td", activated[g], mlp_low[g], preferred_element_type=f32
        )

    def scattered(grad, dim):
        return lax.psum_scatter(
            grad.astype(jnp.bfloat16), "shard", scatter_dimension=dim, tiled=True
        )

    expand_part = scattered(expand_weight_grad, 0)
    reduce_part = scattered(reduce_weight_grad, 1)

    middle_grad, branch_low, shift_two_grad, scale_two_grad, gate_one_grad = [], [], [], [], []
    output_bias_grad, output_weight_grad = 0.0, 0.0
    grads_in = []
    for g in parts:
        shift_two_grad.append(jnp.sum(hidden_two_grad[g], axis=1))
        scale_two_grad.append(jnp.sum(hidden_two_grad[g] * normed_two[g], axis=1))
        middle_grad.append(
            cotangents[g]
            + normalize_back(
                normed_two[g], inverse_two[g], hidden_two_grad[g] * (1.0 + mods[g][4])
            )
        )
        gate_one_grad.append(jnp.sum(middle_grad[g] * branch[g], axis=1))
        branch_grad = middle_grad[g] * mods[g][2]
        output_bias_grad += jnp.sum(branch_grad, axis=(0, 1))
        branch_low.append(branch_grad.astype(jnp.bfloat16))
        attended_grad = jnp.einsum(
            "lsm,fm->lfs", branch_low[g], full_output, preferred_element_type=f32
        ).astype(jnp.bfloat16)
        grads_in.append(to_heads(attended_grad[:, None])[:, 0])
        output_weight_grad += jnp.einsum(
            "lfs,lsk->fk", attended[g], branch_low[g], preferred_element_type=f32
        )
    output_part = scattered(output_weight_grad, 1)

    stacked = []
    for g in parts:
        pulled = attend_back(
            heads_in[g][:, 0], heads_in[g][:, 1], heads_in[g][:, 2], grads_in[g], logsum[g]
        )
        stacked.append(from_heads(jnp.stack(pulled, axis=1)))

    hidden_one_grad, tokens_grad, shift_one_grad, scale_one_grad = [], [], [], []
    project_weight_grad, project_bias_grad = 0.0, 0.0
    for g in parts:
        hidden_one_grad.append(
            tensor_total(
                jnp.einsum("lcfs,dcf->lsd", stacked[g], full_project, preferred_element_type=f32)
            )
        )
    for g in parts:
        project_weight_grad += jnp.einsum(
            "lsd,lcfs->dcf", hidden_one[g], stacked[g], preferred_element_type=f32
        )
        project_bias_grad += jnp.sum(stacked[g].astype(f32), axis=(0, 3))[0::2]
    project_part = scattered(project_weight_grad, 0)
    for g in parts:
        shift_one_grad.append(jnp.sum(hidden_one_grad[g], axis=1))
        scale_one_grad.append(jnp.sum(hidden_one_grad[g] * normed_one[g], axis=1))
        tokens_grad.append(
            middle_grad[g]
            + normalize_back(
                normed_one[g], inverse_one[g], hidden_one_grad[g] * (1.0 + mods[g][1])
            )
        )

    def whole(pieces):
        return jnp.concatenate(pieces, axis=0)

    modulation_grad = jnp.stack(
        [
            whole(shift_one_grad),
            whole(scale_one_grad),
            whole(gate_one_grad),
            whole(shift_two_grad),
            whole(scale_two_grad),
            whole(gate_two_grad),
        ],
        axis=1,
    ).reshape(latents_dev, 6 * width)
    own_columns = lax.dynamic_slice_in_dim(
        modulation_grad, tp_index * half_columns, half_columns, 1
    )
    bias_parts = (project_bias_grad, output_bias_grad, expand_bias_grad, reduce_bias_grad)
    sums = lax.psum(
        jnp.concatenate([own_columns.reshape(-1)] + [part.reshape(-1) for part in bias_parts]),
        "ctx",
    )
    sums = lax.all_gather(sums, "shard", axis=0)
    columns = sums[:, : own_columns.size].reshape(shard_count * latents_dev, half_columns)
    bias_sums = jnp.sum(sums[:, own_columns.size :], axis=0)
    bias_totals = []
    offset = 0
    for part in bias_parts:
        bias_totals.append(bias_sums[offset : offset + part.size].reshape(part.shape))
        offset += part.size
    modulate_bias_share = own_piece(jnp.sum(columns, axis=0), modulate_bias, 0, shard_index)
    project_bias_share = own_piece(bias_totals[0], project_bias, 1, shard_index)
    output_bias_share = own_piece(bias_totals[1], output_bias, 0, shard_index)
    expand_bias_share = own_piece(bias_totals[2], expand_bias, 0, shard_index)
    reduce_bias_share = own_piece(bias_totals[3], reduce_bias, 0, shard_index)

    columns_low = columns.astype(jnp.bfloat16)
    modulate_weight_share = jnp.einsum(
        "ld,lf->df", own_silu, columns_low, preferred_element_type=f32
    )
    silu_part = jnp.einsum("lf,df->ld", columns_low, modulate_weight, preferred_element_type=f32)
    silu_all = jnp.sum(lax.all_gather(silu_part, ("tp", "shard"), axis=0).reshape(
        -1, shard_count, shard_count, latents_dev, depth
    ), axis=0)
    silu_own = lax.dynamic_index_in_dim(silu_all, shard_index, 1, keepdims=False)
    silu_grad = jnp.moveaxis(silu_own, 0, 1).reshape(latents_dev, width)
    unused_silu, silu_pull = jax.vjp(jax.nn.silu, condition.astype(f32))
    condition_grad = silu_pull(silu_grad)[0]

    shares = [
        lax.psum(part, "ctx").astype(f32)
        for part in (project_part, output_part, expand_part, reduce_part)
    ]
    return (
        whole(result),
        whole(tokens_grad),
        condition_grad,
        modulate_weight_share,
        modulate_bias_share,
        shares[0],
        project_bias_share,
        shares[1],
        output_bias_share,
        shares[2],
        expand_bias_share,
        shares[3],
        reduce_bias_share,
    )


def solution(mesh):
    return jax.shard_map(
        shards,
        mesh=mesh,
        in_specs=(
            P("shard", "ctx", None),
            P("shard", None),
            P("shard", "tp"),
            P(("tp", "shard")),
            P("shard", None, "tp"),
            P(None, ("tp", "shard")),
            P("tp", "shard"),
            P("shard"),
            P("shard", "tp"),
            P(("tp", "shard")),
            P("tp", "shard"),
            P("shard"),
            P("shard", "ctx", None),
        ),
        out_specs=(
            P("shard", "ctx", None),
            P("shard", "ctx", None),
            P("shard", None),
            P("shard", "tp"),
            P(("tp", "shard")),
            P("shard", None, "tp"),
            P(None, ("tp", "shard")),
            P("tp", "shard"),
            P("shard"),
            P("shard", "tp"),
            P(("tp", "shard")),
            P("tp", "shard"),
            P("shard"),
        ),
        check_vma=False,
    )
```

```python
from functools import partial

import jax
import jax.numpy as jnp
from jax import lax
from jax.experimental import pallas as pl
from jax.experimental.pallas import tpu as pltpu
from jax.sharding import PartitionSpec as P

HEAD_DIM = 72


epsilon = 1e-06


def normalize(rows):
    average = jnp.mean(rows, axis=-1, keepdims=True)
    centred = rows - average
    variance = jnp.mean(centred * centred, axis=-1, keepdims=True)
    inverse = lax.rsqrt(variance + epsilon)
    return (centred * inverse, inverse)


def normalize_back(normed, inverse, grad_normed):
    first = jnp.mean(grad_normed, axis=-1, keepdims=True)
    second = jnp.mean(grad_normed * normed, axis=-1, keepdims=True)
    return inverse * (grad_normed - first - normed * second)


GROUPS = 2
QUERY_BLOCK = 256
SCALE = HEAD_DIM ** (-0.5)


def after(value, *others):
    return lax.optimization_barrier((value,) + others)[0]


def tensor_totals(partials, last=()):
    count = lax.axis_size("tp")
    own = [part.astype(jnp.bfloat16) for part in partials]
    totals = []
    for g, half in enumerate(own):
        total = half.astype(jnp.float32)
        for step in range(1, count):
            other = lax.ppermute(half, "tp", [(i, (i + step) % count) for i in range(count)])
            if g + 1 < len(own):
                other = after(other, own[g + 1])
            elif last:
                other = after(other, *last)
            total = total + other.astype(jnp.float32)
        totals.append(total)
    return totals


def everyone(value, axis):
    count = lax.axis_size(axis)
    pieces = [value]
    for step in range(1, count):
        pieces.append(lax.ppermute(value, axis, [(i, (i - step) % count) for i in range(count)]))
    twice = jnp.stack(pieces + pieces[:-1])
    start = lax.rem(count - lax.axis_index(axis), count)
    return lax.dynamic_slice_in_dim(twice, start, count, 0)


def contract(left, right, left_dim, right_dim):
    return lax.dot_general(
        left, right, (((left_dim,), (right_dim,)), ((), ())), preferred_element_type=jnp.float32
    )


def attend_kernel(query_ref, key_ref, value_ref, mixed_ref, logsum_ref):
    keys = key_ref[0, 0]
    values = value_ref[0, 0]
    total_queries = query_ref.shape[3]
    for start in range(0, total_queries, QUERY_BLOCK):
        span = slice(start, start + QUERY_BLOCK)
        scores = contract(keys, query_ref[0, 0, :, span], 0, 0) * SCALE
        peak = jnp.max(scores, axis=0, keepdims=True)
        raised = jnp.exp(scores - peak)
        totals = jnp.sum(raised, axis=0, keepdims=True)
        mixed = contract(values, raised.astype(jnp.bfloat16), 1, 0)
        mixed_ref[0, 0, :, span] = (mixed / totals).astype(jnp.bfloat16)
        logsum_ref[0, 0, :, span] = peak + jnp.log(totals)


def attend_back_kernel(
    query_ref, key_ref, value_ref, grad_ref, logsum_ref, query_out, key_out, value_out
):
    keys = key_ref[0, 0]
    values = value_ref[0, 0]
    total_queries = query_ref.shape[3]
    key_total = jnp.zeros(keys.shape, jnp.float32)
    value_total = jnp.zeros(keys.shape, jnp.float32)
    for start in range(0, total_queries, QUERY_BLOCK):
        span = slice(start, start + QUERY_BLOCK)
        query = query_ref[0, 0, :, span]
        grad = grad_ref[0, 0, :, span]
        scores = contract(keys, query, 0, 0) * SCALE
        probs = jnp.exp(scores - logsum_ref[0, 0, :, span])
        prob_grad = contract(values, grad, 0, 0)
        row_dot = jnp.sum(probs * prob_grad, axis=0, keepdims=True)
        score_grad = (probs * (prob_grad - row_dot) * SCALE).astype(jnp.bfloat16)
        value_total += contract(grad, probs.astype(jnp.bfloat16), 1, 1)
        key_total += contract(query, score_grad, 1, 1)
        query_out[0, 0, :, span] = contract(keys, score_grad, 1, 0).astype(jnp.bfloat16)
    key_out[0, 0] = key_total.astype(jnp.bfloat16)
    value_out[0, 0] = value_total.astype(jnp.bfloat16)


def head_spec(rows, columns):
    return pl.BlockSpec((1, 1, rows, columns), lambda l, h: (l, h, 0, 0))


def attend(queries, keys, values):
    latents, heads, features, count = queries.shape
    wide = head_spec(features, count)
    thin = head_spec(1, count)
    return pl.pallas_call(
        attend_kernel,
        grid=(latents, heads),
        in_specs=[wide] * 3,
        out_specs=[wide, thin],
        out_shape=[
            jax.ShapeDtypeStruct(queries.shape, jnp.bfloat16),
            jax.ShapeDtypeStruct((latents, heads, 1, count), jnp.float32),
        ],
        compiler_params=pltpu.CompilerParams(vmem_limit_bytes=40 * 2**20),
        cost_estimate=pl.CostEstimate(
            flops=4 * latents * heads * 256 * count * count,
            bytes_accessed=8 * queries.size,
            transcendentals=latents * heads * count * count,
        ),
    )(queries, keys, values)


def attend_back(queries, keys, values, grads, logsum):
    latents, heads, features, count = queries.shape
    wide = head_spec(features, count)
    thin = head_spec(1, count)
    return pl.pallas_call(
        attend_back_kernel,
        grid=(latents, heads),
        in_specs=[wide] * 4 + [thin],
        out_specs=[wide] * 3,
        out_shape=[jax.ShapeDtypeStruct(queries.shape, jnp.bfloat16)] * 3,
        compiler_params=pltpu.CompilerParams(vmem_limit_bytes=40 * 2**20),
        cost_estimate=pl.CostEstimate(
            flops=10 * latents * heads * 256 * count * count,
            bytes_accessed=14 * queries.size,
            transcendentals=latents * heads * count * count,
        ),
    )(queries, keys, values, grads, logsum)


def to_heads(rows_in, following=None):
    count = lax.axis_size("ctx")
    me = lax.axis_index("ctx")
    latents, kinds, features, own = rows_in.shape
    split = rows_in.reshape(latents, kinds, count, features // (count * HEAD_DIM), HEAD_DIM, own)
    blocks = []
    for step in range(count):
        piece = lax.dynamic_index_in_dim(split, lax.rem(me + step, count), 2, keepdims=False)
        if step:
            piece = lax.ppermute(piece, "ctx", [(i, (i + step) % count) for i in range(count)])
            if following is not None:
                piece = after(piece, following)
        blocks.append(piece)
    return jnp.concatenate(blocks, axis=-1)


def from_heads(blocks_in, following=None):
    count = lax.axis_size("ctx")
    me = lax.axis_index("ctx")
    latents, kinds, heads, features, total = blocks_in.shape
    own = total // count
    pieces = []
    for step in range(count):
        piece = blocks_in[..., step * own : (step + 1) * own]
        if step:
            piece = lax.ppermute(piece, "ctx", [(i, (i - step) % count) for i in range(count)])
            if following is not None:
                piece = after(piece, following)
        pieces.append(piece)
    twice = jnp.stack(pieces + pieces[:-1], axis=2)
    placed = lax.dynamic_slice_in_dim(twice, lax.rem(count - me, count), count, 2)
    return placed.reshape(latents, kinds, count * heads * features, own)


def pipelined(transfer, values):
    return [transfer(*pair) for pair in zip(values, values[1:] + [None])]


def own_piece(total, local, dim, shard_index):
    count = local.shape[dim]
    return lax.dynamic_slice_in_dim(total, shard_index * count, count, dim)


def shards(
    tokens,
    condition,
    modulate_weight,
    modulate_bias,
    project_weight,
    project_bias,
    output_weight,
    output_bias,
    expand_weight,
    expand_bias,
    reduce_weight,
    reduce_bias,
    cotangent,
):
    tp_index = lax.axis_index("tp")
    shard_index = lax.axis_index("shard")
    shard_count = lax.axis_size("shard")
    latents_dev = tokens.shape[0]
    width = tokens.shape[2]
    depth = modulate_weight.shape[0]
    half_columns = modulate_weight.shape[1]
    f32 = jnp.float32

    small = (condition, modulate_bias, project_bias, output_bias, expand_bias, reduce_bias)
    packed = everyone(jnp.concatenate([part.reshape(-1) for part in small]), "shard")
    offset = 0
    unpacked = []
    for part in small:
        unpacked.append(packed[:, offset : offset + part.size].reshape((shard_count,) + part.shape))
        offset += part.size
    full_condition = unpacked[0].reshape(shard_count * latents_dev, width)
    full_modulate_bias = unpacked[1].reshape(-1)
    full_project_bias = jnp.moveaxis(unpacked[2], 0, 1).reshape(2, -1).astype(f32)
    full_output_bias = unpacked[3].reshape(-1).astype(f32)
    full_expand_bias = unpacked[4].reshape(-1).astype(f32)
    full_reduce_bias = unpacked[5].reshape(-1).astype(f32)

    full_project = lax.all_gather(project_weight, "shard", axis=0, tiled=True)
    full_output = lax.all_gather(output_weight, "shard", axis=1, tiled=True)
    full_expand = lax.all_gather(expand_weight, "shard", axis=0, tiled=True)
    full_reduce = lax.all_gather(reduce_weight, "shard", axis=1, tiled=True)

    silu_cond = jax.nn.silu(full_condition.astype(f32)).astype(jnp.bfloat16)
    own_silu = lax.dynamic_slice_in_dim(silu_cond, shard_index * depth, depth, 1)
    modulate_part = jnp.dot(own_silu, modulate_weight, preferred_element_type=f32)
    by_owner = modulate_part.reshape(shard_count, latents_dev, half_columns)
    modulate_half = full_modulate_bias.astype(f32) + lax.dynamic_index_in_dim(
        by_owner, shard_index, 0, keepdims=False
    )
    for step in range(1, shard_count):
        piece = lax.dynamic_index_in_dim(
            by_owner, lax.rem(shard_index + step, shard_count), 0, keepdims=False
        )
        modulate_half = modulate_half + lax.ppermute(
            piece, "shard", [(i, (i + step) % shard_count) for i in range(shard_count)]
        )
    modulation = jnp.moveaxis(everyone(modulate_half, "tp"), 0, 1).reshape(latents_dev, 6, width)

    groups = GROUPS if latents_dev % GROUPS == 0 else 1
    size = latents_dev // groups
    spans = [slice(g * size, (g + 1) * size) for g in range(groups)]
    parts = range(groups)
    mods = [[modulation[s, i][:, None, :] for i in range(6)] for s in spans]
    inputs = [tokens[s].astype(f32) for s in spans]
    cotangents = [cotangent[s] for s in spans]

    normed_one, inverse_one, hidden_one, projections = [], [], [], []
    for g in parts:
        normed, inverse = normalize(inputs[g])
        normed_one.append(normed)
        inverse_one.append(inverse)
        hidden_one.append((normed * (1.0 + mods[g][1]) + mods[g][0]).astype(jnp.bfloat16))
        projected = jnp.einsum(
            "lsd,dcf->lcfs", hidden_one[g], full_project, preferred_element_type=f32
        )
        bias = jnp.stack(
            [full_project_bias[0], jnp.zeros_like(full_project_bias[0]), full_project_bias[1]]
        )
        projections.append((projected + bias[None, :, :, None]).astype(jnp.bfloat16))
    heads_in = pipelined(to_heads, projections)

    logsum, mixes = [], []
    for g in parts:
        mixed, log_one = attend(heads_in[g][:, 0], heads_in[g][:, 1], heads_in[g][:, 2])
        logsum.append(log_one)
        mixes.append(mixed[:, None])
    attended = [mixed[:, 0] for mixed in pipelined(from_heads, mixes)]

    middle, normed_two, inverse_two, hidden_two = [], [], [], []
    branch = tensor_totals(
        [
            jnp.einsum("lfs,fk->lsk", attended[g], full_output, preferred_element_type=f32)
            for g in parts
        ]
    )
    branch = [total + full_output_bias for total in branch]
    for g in parts:
        middle.append(inputs[g] + mods[g][2] * branch[g])
        normed, inverse = normalize(middle[g])
        normed_two.append(normed)
        inverse_two.append(inverse)
        hidden_two.append((normed * (1.0 + mods[g][4]) + mods[g][3]).astype(jnp.bfloat16))

    mlp_low, expand_low, result, activated, hidden_two_part = [], [], [], [], []
    gate_two_grad, reduce_bias_grad, expand_bias_grad = [], 0.0, 0.0
    expand_weight_grad, reduce_weight_grad = 0.0, 0.0
    for g in parts:
        mlp_grad = cotangents[g] * mods[g][5]
        reduce_bias_grad += jnp.sum(mlp_grad, axis=(0, 1))
        mlp_low.append(mlp_grad.astype(jnp.bfloat16))
        inner = (
            jnp.einsum("lsd,dt->lst", hidden_two[g], full_expand, preferred_element_type=f32)
            + full_expand_bias
        )
        gelu = partial(jax.nn.gelu, approximate=True)
        activated.append(gelu(inner).astype(jnp.bfloat16))
        activated_grad = jnp.einsum(
            "lsd,td->lst", mlp_low[g], full_reduce, preferred_element_type=f32
        )
        unused_value, gelu_pull = jax.vjp(gelu, inner)
        inner_grad = gelu_pull(activated_grad)[0]
        expand_bias_grad += jnp.sum(inner_grad, axis=(0, 1))
        expand_low.append(inner_grad.astype(jnp.bfloat16))
        hidden_two_part.append(
            jnp.einsum("lst,dt->lsd", expand_low[g], full_expand, preferred_element_type=f32)
        )
    for g in parts:
        expand_weight_grad += jnp.einsum(
            "lsd,lst->dt", hidden_two[g], expand_low[g], preferred_element_type=f32
        )
        reduce_weight_grad += jnp.einsum(
            "lst,lsd->td", activated[g], mlp_low[g], preferred_element_type=f32
        )

    def scattered(grad, dim):
        return lax.psum_scatter(grad, "shard", scatter_dimension=dim, tiled=True)

    expand_weight_grad = expand_weight_grad.astype(jnp.bfloat16)
    reduce_weight_grad = reduce_weight_grad.astype(jnp.bfloat16)
    hidden_two_grad = tensor_totals(hidden_two_part, (expand_weight_grad, reduce_weight_grad))
    expand_part = scattered(expand_weight_grad, 0)
    reduce_part = scattered(reduce_weight_grad, 1)

    middle_grad, branch_low, shift_two_grad, scale_two_grad, gate_one_grad = [], [], [], [], []
    output_bias_grad, output_weight_grad = 0.0, 0.0
    grads_in = []
    for g in parts:
        shift_two_grad.append(jnp.sum(hidden_two_grad[g], axis=1))
        scale_two_grad.append(jnp.sum(hidden_two_grad[g] * normed_two[g], axis=1))
        middle_grad.append(
            cotangents[g]
            + normalize_back(
                normed_two[g], inverse_two[g], hidden_two_grad[g] * (1.0 + mods[g][4])
            )
        )
        gate_one_grad.append(jnp.sum(middle_grad[g] * branch[g], axis=1))
        branch_grad = middle_grad[g] * mods[g][2]
        output_bias_grad += jnp.sum(branch_grad, axis=(0, 1))
        branch_low.append(branch_grad.astype(jnp.bfloat16))
        attended_grad = jnp.einsum(
            "lsm,fm->lfs", branch_low[g], full_output, preferred_element_type=f32
        ).astype(jnp.bfloat16)
        grads_in.append(attended_grad[:, None])
        output_weight_grad += jnp.einsum(
            "lfs,lsk->fk", attended[g], branch_low[g], preferred_element_type=f32
        )
    output_part = scattered(output_weight_grad.astype(jnp.bfloat16), 1)
    early = [lax.psum(part, "ctx") for part in (output_part, expand_part, reduce_part)]

    mlp_out = tensor_totals(
        [
            jnp.einsum(
                "lst,td->lsd",
                after(activated[g], grads_in[-1]),
                full_reduce,
                preferred_element_type=f32,
            )
            for g in parts
        ]
    )
    mlp_out = [total + full_reduce_bias for total in mlp_out]
    grads_in = [grad[:, 0] for grad in pipelined(to_heads, grads_in)]

    pulls = []
    for g in parts:
        pulled = attend_back(
            heads_in[g][:, 0], heads_in[g][:, 1], heads_in[g][:, 2], grads_in[g], logsum[g]
        )
        pulls.append(jnp.stack(pulled, axis=1))
    stacked = pipelined(from_heads, pulls)
    for g in parts:
        result.append(middle[g] + mods[g][5] * mlp_out[g])
        gate_two_grad.append(jnp.sum(cotangents[g] * mlp_out[g], axis=1))

    tokens_grad, shift_one_grad, scale_one_grad = [], [], []
    project_weight_grad, project_bias_grad = 0.0, 0.0
    for g in parts:
        project_weight_grad += jnp.einsum(
            "lsd,lcfs->dcf", hidden_one[g], stacked[g], preferred_element_type=f32
        )
        project_bias_grad += jnp.sum(stacked[g].astype(f32), axis=(0, 3))[0::2]
    project_weight_grad = project_weight_grad.astype(jnp.bfloat16)
    project_part = scattered(project_weight_grad, 0)
    stacked[-1] = after(stacked[-1], project_weight_grad)
    hidden_one_grad = tensor_totals(
        [
            jnp.einsum("lcfs,dcf->lsd", stacked[g], full_project, preferred_element_type=f32)
            for g in parts
        ]
    )
    for g in parts:
        shift_one_grad.append(jnp.sum(hidden_one_grad[g], axis=1))
        scale_one_grad.append(jnp.sum(hidden_one_grad[g] * normed_one[g], axis=1))
        tokens_grad.append(
            middle_grad[g]
            + normalize_back(
                normed_one[g], inverse_one[g], hidden_one_grad[g] * (1.0 + mods[g][1])
            )
        )

    def whole(pieces):
        return jnp.concatenate(pieces, axis=0)

    modulation_grad = jnp.stack(
        [
            whole(shift_one_grad),
            whole(scale_one_grad),
            whole(gate_one_grad),
            whole(shift_two_grad),
            whole(scale_two_grad),
            whole(gate_two_grad),
        ],
        axis=1,
    ).reshape(latents_dev, 6 * width)
    own_columns = lax.dynamic_slice_in_dim(
        modulation_grad, tp_index * half_columns, half_columns, 1
    )
    bias_parts = (project_bias_grad, output_bias_grad, expand_bias_grad, reduce_bias_grad)
    sums = jnp.concatenate(
        [own_columns.reshape(-1)] + [part.reshape(-1) for part in bias_parts]
    )
    sums = everyone(jnp.sum(everyone(sums, "ctx"), axis=0), "shard")
    columns = sums[:, : own_columns.size].reshape(shard_count * latents_dev, half_columns)
    bias_sums = jnp.sum(sums[:, own_columns.size :], axis=0)
    bias_totals = []
    offset = 0
    for part in bias_parts:
        bias_totals.append(bias_sums[offset : offset + part.size].reshape(part.shape))
        offset += part.size
    modulate_bias_share = own_piece(jnp.sum(columns, axis=0), modulate_bias, 0, shard_index)
    project_bias_share = own_piece(bias_totals[0], project_bias, 1, shard_index)
    output_bias_share = own_piece(bias_totals[1], output_bias, 0, shard_index)
    expand_bias_share = own_piece(bias_totals[2], expand_bias, 0, shard_index)
    reduce_bias_share = own_piece(bias_totals[3], reduce_bias, 0, shard_index)

    columns_low = columns.astype(jnp.bfloat16)
    modulate_weight_share = jnp.einsum(
        "ld,lf->df", own_silu, columns_low, preferred_element_type=f32
    )
    silu_part = jnp.einsum("lf,df->ld", columns_low, modulate_weight, preferred_element_type=f32)
    silu_all = everyone(jnp.sum(everyone(silu_part, "tp"), axis=0), "shard").reshape(
        shard_count, shard_count, latents_dev, depth
    )
    silu_own = lax.dynamic_index_in_dim(silu_all, shard_index, 1, keepdims=False)
    silu_grad = jnp.moveaxis(silu_own, 0, 1).reshape(latents_dev, width)
    unused_silu, silu_pull = jax.vjp(jax.nn.silu, condition.astype(f32))
    condition_grad = silu_pull(silu_grad)[0]

    late = lax.psum(after(project_part, *early), "ctx")
    shares = [part.astype(f32) for part in [late] + early]
    return (
        whole(result),
        whole(tokens_grad),
        condition_grad,
        modulate_weight_share,
        modulate_bias_share,
        shares[0],
        project_bias_share,
        shares[1],
        output_bias_share,
        shares[2],
        expand_bias_share,
        shares[3],
        reduce_bias_share,
    )


def solution(mesh):
    return jax.shard_map(
        shards,
        mesh=mesh,
        in_specs=(
            P("shard", "ctx", None),
            P("shard", None),
            P("shard", "tp"),
            P(("tp", "shard")),
            P("shard", None, "tp"),
            P(None, ("tp", "shard")),
            P("tp", "shard"),
            P("shard"),
            P("shard", "tp"),
            P(("tp", "shard")),
            P("tp", "shard"),
            P("shard"),
            P("shard", "ctx", None),
        ),
        out_specs=(
            P("shard", "ctx", None),
            P("shard", "ctx", None),
            P("shard", None),
            P("shard", "tp"),
            P(("tp", "shard")),
            P("shard", None, "tp"),
            P(None, ("tp", "shard")),
            P("tp", "shard"),
            P("shard"),
            P("shard", "tp"),
            P(("tp", "shard")),
            P("tp", "shard"),
            P("shard"),
        ),
        check_vma=False,
    )
```
